32 devices in a mesh: inp: 4 (over z), chan: 8 (over y, x, core).
Axes of the slice: x: 2, y: 2, z: 4, core: 2. Of those that a mesh axis runs over, the one named last changes fastest.
Arguments:
- samples: bfloat16 [1024, 128, 512], P('inp', 'chan'), may hold values from -16 to 16
- gram_owner: int32 [128], replicated, may hold values from 0 to 31, as said below
- beam_owner: int32 [256], replicated, may hold values from 0 to 7, as said below
- delays: float32 [256, 1024], replicated, may hold values from -64 to 64
- sections: int32 [256], replicated, may hold values from 0 to 255, each once
Outputs:
- visibilities: float32 [256, 2, 1024, 1024], P(('inp', 'chan'))
- beam_voltages: float32 [512, 4, 128, 128], P('chan', 'inp')
The draws below stay inside these ranges and needn't reach their ends.
Inputs may be any that keep to these rules, and one draw needn't show every extreme that they name: `gram_owner`: no device owns more than 8 of the correlated channels, and some device owns exactly 8. `beam_owner`: no index of chan owns more than 64 channels, and some owns exactly 64. `sections`: each value once.
All inputs are finite; a program needn't handle non-finite values.
Results may differ from the reference program's by a relative error of at most 0.0048.
Values may be sent and summed in bfloat16 or wider, within the bound.
A program may use at most 256 MiB of HBM per device.

```python
import math
import jax
import jax.numpy as jnp
from jax import lax

WIDTH = 512
NCH = 256
XCH = 128
NIN = 1024
NBEAM = 256
FRAMES = 128
B_SEC = 64
XOWNERS = 32
XSLOTS = 8
BSLOTS = 64
N_INP = 4
N_CHAN = 8


def allot_owners(key, owner_count, slot_count, count):
    first_key, second_key, third_key = jax.random.split(key, 3)
    full_owner = jax.random.randint(first_key, (), 0, owner_count)
    order = jax.random.permutation(second_key, owner_count * slot_count)
    taken = (order // slot_count == full_owner).astype(jnp.int32)
    ranking = jnp.argsort(taken * (owner_count * slot_count) + jnp.arange(owner_count * slot_count), stable=True)
    remaining = order[ranking]
    picked = jnp.concatenate([full_owner * slot_count + jnp.arange(slot_count), remaining[:count - slot_count]])
    shuffle = jax.random.permutation(third_key, count)
    return (picked[shuffle] // slot_count).astype(jnp.int32)


def draw_gram_owner(key, part):
    return allot_owners(jax.random.fold_in(key, 11), XOWNERS, XSLOTS, XCH)


def draw_beam_owner(key, part):
    return allot_owners(jax.random.fold_in(key, 23), N_CHAN, BSLOTS, NCH)


def draw_samples(key, part):
    sky_key, gain_key, noise_key = jax.random.split(jax.random.fold_in(key, 37), 3)
    sky = jnp.clip(jax.random.normal(sky_key, (1, FRAMES, WIDTH), jnp.float32), -5.0, 5.0)
    gains = jax.random.uniform(gain_key, (NIN, 1, 1), jnp.float32, -1.5, 1.5)
    noise = jnp.clip(jax.random.normal(noise_key, (NIN, FRAMES, WIDTH), jnp.float32), -5.0, 5.0)
    return (gains * sky + noise).astype(jnp.bfloat16)


def setup_inputs(seed: int = 0) -> dict:
    seeds = jax.random.split(jax.random.key(seed), 6)
    return {
        "samples": draw_samples(jax.random.fold_in(seeds[5], 71), 0),
        "gram_owner": draw_gram_owner(jax.random.fold_in(seeds[5], 71), 0),
        "beam_owner": draw_beam_owner(jax.random.fold_in(seeds[5], 71), 0),
        "delays": jnp.clip(jax.random.uniform(seeds[3], (NBEAM, NIN), jnp.float32, -64.0, 64.0), -64.0, 64.0),
        "sections": jax.random.permutation(seeds[4], NBEAM).astype(jnp.int32),
    }


def fourier_table(length_total):
    half_count = length_total // 2
    rows = jnp.arange(half_count, dtype=jnp.int32)
    cols = jnp.arange(length_total, dtype=jnp.int32)
    turns = (rows[:, None] * cols[None, :] % length_total).astype(jnp.float32) * (2.0 * math.pi / length_total)
    factor = 1.0 / math.sqrt(length_total)
    return jnp.stack([jnp.cos(turns) * factor, -jnp.sin(turns) * factor]).astype(jnp.bfloat16)

def slot_table(owner_list, owner_count, slot_count):
    count = owner_list.shape[0]
    places = jnp.arange(count, dtype=jnp.int32)
    before = (owner_list[None, :] == owner_list[:, None]) & (places[None, :] < places[:, None])
    slot_of = lax.optimization_barrier(jnp.sum(before.astype(jnp.int32), axis=1)).astype(jnp.int32)
    keys = (owner_list * slot_count + slot_of).astype(jnp.int32)
    targets = jnp.arange(owner_count * slot_count, dtype=jnp.int32)
    match = keys[None, :] == targets[:, None]
    channel_of = lax.optimization_barrier(jnp.sum(jnp.where(match, places[None, :], 0), axis=1)).astype(jnp.int32)
    live_slot = jnp.any(match, axis=1)
    return (keys, channel_of, live_slot)

def reference(samples, gram_owner, beam_owner, delays, sections):
    table = fourier_table(WIDTH)
    spectra = jnp.einsum('pkw,ifw->kpfi', table.astype(jnp.float32), samples.astype(jnp.float32)).astype(jnp.bfloat16)
    gram_keys, _, _ = slot_table(gram_owner, XOWNERS, XSLOTS)

    def correlate(index):
        block = spectra[index]
        real_rows = block[0]
        imag_rows = block[1]
        real_part = jnp.dot(real_rows.T, real_rows, preferred_element_type=jnp.float32) + jnp.dot(imag_rows.T, imag_rows, preferred_element_type=jnp.float32)
        imag_part = jnp.dot(imag_rows.T, real_rows, preferred_element_type=jnp.float32) - jnp.dot(real_rows.T, imag_rows, preferred_element_type=jnp.float32)
        return jnp.stack([real_part, imag_part]) / FRAMES
    grams = lax.map(correlate, jnp.arange(XCH, dtype=jnp.int32))
    visibilities = jnp.zeros((XOWNERS * XSLOTS, 2, NIN, NIN), jnp.float32).at[gram_keys].set(grams)
    beam_keys, _, _ = slot_table(beam_owner, N_CHAN, BSLOTS)
    inverse = 1.0 / math.sqrt(NIN)

    def form(index):
        block = spectra[index]
        frequency = index.astype(jnp.float32)
        angle = frequency * delays * (2.0 * math.pi / WIDTH)
        real_weight = (jnp.cos(angle) * inverse).astype(jnp.bfloat16)
        imag_weight = (-jnp.sin(angle) * inverse).astype(jnp.bfloat16)
        real_beam = jnp.dot(block[0], real_weight.T, preferred_element_type=jnp.float32) - jnp.dot(block[1], imag_weight.T, preferred_element_type=jnp.float32)
        imag_beam = jnp.dot(block[1], real_weight.T, preferred_element_type=jnp.float32) + jnp.dot(block[0], imag_weight.T, preferred_element_type=jnp.float32)
        both = jnp.stack([real_beam, imag_beam], axis=1)
        both = jnp.take(both, sections, axis=2).reshape(FRAMES, 2, N_INP, B_SEC)
        return jnp.transpose(both, (2, 0, 1, 3)).reshape(N_INP, FRAMES, 2 * B_SEC)
    formed = lax.map(form, jnp.arange(NCH, dtype=jnp.int32))
    beam_voltages = jnp.zeros((N_CHAN * BSLOTS, N_INP, FRAMES, 2 * B_SEC), jnp.float32).at[beam_keys].set(formed)
    return (visibilities, beam_voltages)
```

```python
import functools
import math

import jax
import jax.numpy as jnp
import numpy as np
from jax import lax
from jax.experimental import pallas as pl
from jax.experimental.pallas import tpu as pltpu
from jax.sharding import PartitionSpec as P

VMEM_BYTES = 56 * 1024 * 1024


def fourier_table(length_total):
    half_count = length_total // 2
    rows = np.arange(half_count, dtype=np.int32)
    cols = np.arange(length_total, dtype=np.int32)
    turns = (rows[:, None] * cols[None, :] % length_total).astype(np.float32) * np.float32(
        2.0 * math.pi / length_total
    )
    factor = np.float32(1.0 / math.sqrt(length_total))
    table = np.stack([np.cos(turns) * factor, -np.sin(turns) * factor], axis=1)
    return jnp.asarray(table.astype(jnp.bfloat16))


def slot_table(owner_list, owner_count, slot_count):
    count = owner_list.shape[0]
    places = jnp.arange(count, dtype=jnp.int32)
    before = (owner_list[None, :] == owner_list[:, None]) & (places[None, :] < places[:, None])
    slot_of = jnp.sum(before.astype(jnp.int32), axis=1)
    keys = owner_list * slot_count + slot_of
    targets = jnp.arange(owner_count * slot_count, dtype=jnp.int32)
    match = keys[None, :] == targets[:, None]
    channel_of = jnp.sum(jnp.where(match, places[None, :], 0), axis=1)
    live_slot = jnp.any(match, axis=1)
    return channel_of, live_slot


def gram_kernel(scale, data_ref, out_ref):
    inps, chans, _, _, frames, width = data_ref.shape
    parts = []
    for part in range(2):
        blocks = [
            data_ref[z, :, 0, part].reshape(chans * frames, width) for z in range(inps)
        ]
        parts.append(jnp.concatenate(blocks, axis=1))
    real, imag = parts
    both = jnp.concatenate([real, imag], axis=0)
    turned = jnp.concatenate([imag, -real], axis=0)
    tile = out_ref.shape[2]
    for lhs, part in ((both, 0), (turned, 1)):
        for row in range(0, tile, 256):
            out_ref[0, part, row : row + 256] = (
                lax.dot_general(
                    lhs[:, row : row + 256],
                    both,
                    (((0,), (0,)), ((), ())),
                    preferred_element_type=jnp.float32,
                )
                * scale
            )


def correlate(arrived, frames_total):
    inps, chans, slots, _, frames, width = arrived.shape
    total = inps * width
    return pl.pallas_call(
        functools.partial(gram_kernel, 1.0 / frames_total),
        grid=(slots,),
        in_specs=[
            pl.BlockSpec((inps, chans, 1, 2, frames, width), lambda s: (0, 0, s, 0, 0, 0))
        ],
        out_specs=pl.BlockSpec((1, 2, total, total), lambda s: (s, 0, 0, 0)),
        out_shape=jax.ShapeDtypeStruct((slots, 2, total, total), jnp.float32),
        compiler_params=pltpu.CompilerParams(vmem_limit_bytes=VMEM_BYTES),
        cost_estimate=pl.CostEstimate(
            flops=slots * 2 * 2 * total * total * 2 * chans * frames,
            bytes_accessed=slots * 2 * total * total * 4,
            transcendentals=0,
        ),
    )(arrived)


SIN_TERMS = [
    (-1) ** n * (2 * math.pi) ** (2 * n + 1) / math.factorial(2 * n + 1) for n in range(9)
]
COS_TERMS = [(-1) ** n * (2 * math.pi) ** (2 * n) / math.factorial(2 * n) for n in range(10)]


def turn_pair(turns):
    rest = turns - jnp.round(turns)
    square = rest * rest
    sine = jnp.full_like(square, SIN_TERMS[-1])
    for term in SIN_TERMS[-2::-1]:
        sine = sine * square + term
    cosine = jnp.full_like(square, COS_TERMS[-1])
    for term in COS_TERMS[-2::-1]:
        cosine = cosine * square + term
    return cosine, sine * rest


def beam_kernel(chan_axis, length_total, inverse, data_ref, delay_ref, out_ref, state, step):
    index = pl.program_id(0)
    chans, _, _, frames, width = data_ref.shape
    sects = out_ref.shape[0]
    beams = delay_ref.shape[1]

    @pl.when(index == 0)
    def _():
        first = (lax.axis_index(chan_axis) * pl.num_programs(0)).astype(jnp.float32)

        @pl.loop(0, width, step=32)
        def _(row):
            rows = pl.ds(pl.multiple_of(row, 32), 32)
            delay = delay_ref[rows]
            scaled = delay * (1.0 / length_total)
            cosine, sine = turn_pair(scaled)
            step[0, rows] = cosine
            step[1, rows] = -sine
            cosine, sine = turn_pair((first * delay) * (1.0 / length_total))
            state[0, rows] = cosine * inverse
            state[1, rows] = -sine * inverse

    real_state = state[0]
    imag_state = state[1]
    real_weight = real_state.astype(jnp.bfloat16)
    imag_weight = imag_state.astype(jnp.bfloat16)
    real_step = step[0]
    imag_step = step[1]
    state[0] = real_state * real_step - imag_state * imag_step
    state[1] = real_state * imag_step + imag_state * real_step
    half = chans * frames
    data = jnp.concatenate(
        [data_ref[:, 0, 0].reshape(half, width), data_ref[:, 0, 1].reshape(half, width)], axis=0
    )
    by_real = jnp.dot(data, real_weight, preferred_element_type=jnp.float32)
    by_imag = jnp.dot(data, imag_weight, preferred_element_type=jnp.float32)
    real_beam = by_real[:half] - by_imag[half:]
    imag_beam = by_real[half:] + by_imag[:half]
    span = beams // sects
    for sect in range(sects):
        cols = slice(sect * span, (sect + 1) * span)
        out_ref[sect, 0] = jnp.concatenate([real_beam[:, cols], imag_beam[:, cols]], axis=1).astype(
            out_ref.dtype
        )


def form_beams(data, delays, length_total, all_inputs, sects):
    chans, held, _, frames, width = data.shape
    beams = delays.shape[1]
    span = beams // sects
    return pl.pallas_call(
        functools.partial(beam_kernel, "chan", length_total, 1.0 / math.sqrt(all_inputs)),
        grid=(held,),
        in_specs=[
            pl.BlockSpec((chans, 1, 2, frames, width), lambda c: (0, c, 0, 0, 0)),
            pl.BlockSpec((width, beams), lambda c: (0, 0)),
        ],
        out_specs=pl.BlockSpec((sects, 1, chans * frames, 2 * span), lambda c: (0, c, 0, 0)),
        out_shape=jax.ShapeDtypeStruct((sects, held, chans * frames, 2 * span), jnp.bfloat16),
        scratch_shapes=[
            pltpu.VMEM((2, width, beams), jnp.float32),
            pltpu.VMEM((2, width, beams), jnp.float32),
        ],
        compiler_params=pltpu.CompilerParams(vmem_limit_bytes=VMEM_BYTES),
        cost_estimate=pl.CostEstimate(
            flops=held * 2 * 4 * chans * frames * width * beams,
            bytes_accessed=held * chans * frames * (4 * width + 4 * beams),
            transcendentals=0,
        ),
    )(data, delays)


def shards(samples, gram_owner, beam_owner, delays, sections):
    input_count, frame_count, length_total = samples.shape
    half_count = length_total // 2
    inp_count = lax.axis_size("inp")
    chan_count = lax.axis_size("chan")
    inp_here = lax.axis_index("inp")
    chan_here = lax.axis_index("chan")
    all_inputs = input_count * inp_count
    all_frames = frame_count * chan_count
    owner_count = inp_count * chan_count
    gram_slots = 2 * gram_owner.shape[0] // owner_count
    beam_slots = 2 * half_count // chan_count
    held = half_count // chan_count
    table = fourier_table(length_total)
    spectra = jnp.einsum(
        "kpw,ifw->kpfi", table, samples, preferred_element_type=jnp.float32
    ).astype(jnp.bfloat16)

    mine = spectra.reshape(chan_count, held, 2, frame_count, input_count)
    beam_data = lax.all_to_all(mine, "chan", split_axis=0, concat_axis=0, tiled=True)

    gram_channel, gram_live = slot_table(gram_owner, owner_count, gram_slots)
    outgoing = jnp.where(
        gram_live[:, None, None, None],
        jnp.take(spectra, gram_channel, axis=0),
        jnp.zeros((), jnp.bfloat16),
    )
    outgoing = outgoing.reshape(owner_count, gram_slots, 2, frame_count, input_count)
    arrived = lax.all_to_all(outgoing, ("inp", "chan"), split_axis=0, concat_axis=0, tiled=True)
    arrived = arrived.reshape(inp_count, chan_count, gram_slots, 2, frame_count, input_count)

    delay_cols = lax.dynamic_slice_in_dim(delays, inp_here * input_count, input_count, 1)
    ordered = jnp.take(delay_cols, sections, axis=0).T
    partial_beams = form_beams(beam_data, ordered, length_total, all_inputs, inp_count)
    terms = lax.all_to_all(partial_beams, "inp", split_axis=0, concat_axis=0, tiled=True)
    formed = jnp.sum(terms.astype(jnp.float32), axis=0).astype(jnp.bfloat16)
    every = lax.all_gather(formed, "chan", axis=0, tiled=True)

    visibilities = correlate(arrived, all_frames)

    beam_channel, beam_live = slot_table(beam_owner, chan_count, beam_slots)
    here = lax.dynamic_slice_in_dim(beam_channel, chan_here * beam_slots, beam_slots)
    live = lax.dynamic_slice_in_dim(beam_live, chan_here * beam_slots, beam_slots)
    voltages = jnp.where(
        live[:, None, None], jnp.take(every, here, axis=0), jnp.zeros((), jnp.bfloat16)
    ).astype(jnp.float32)
    return (visibilities, voltages[:, None])


def solution(mesh):
    return jax.shard_map(
        shards,
        mesh=mesh,
        in_specs=(P("inp", "chan", None), P(), P(), P(), P()),
        out_specs=(P(("inp", "chan"), None, None, None), P("chan", "inp", None, None)),
        check_vma=False,
    )
```

```python
import functools
import math

import jax
import jax.numpy as jnp
import numpy as np
from jax import lax
from jax.experimental import pallas as pl
from jax.experimental.pallas import tpu as pltpu
from jax.sharding import PartitionSpec as P

VMEM_BYTES = 56 * 1024 * 1024


def fourier_table(length_total):
    half_count = length_total // 2
    rows = np.arange(half_count, dtype=np.int32)
    cols = np.arange(length_total, dtype=np.int32)
    turns = (rows[:, None] * cols[None, :] % length_total).astype(np.float32) * np.float32(
        2.0 * math.pi / length_total
    )
    factor = np.float32(1.0 / math.sqrt(length_total))
    table = np.stack([np.cos(turns) * factor, -np.sin(turns) * factor], axis=1)
    return jnp.asarray(table.astype(jnp.bfloat16))


def slot_table(owner_list, owner_count, slot_count):
    count = owner_list.shape[0]
    places = jnp.arange(count, dtype=jnp.int32)
    before = (owner_list[None, :] == owner_list[:, None]) & (places[None, :] < places[:, None])
    slot_of = jnp.sum(before.astype(jnp.int32), axis=1)
    keys = owner_list * slot_count + slot_of
    targets = jnp.arange(owner_count * slot_count, dtype=jnp.int32)
    match = keys[None, :] == targets[:, None]
    channel_of = jnp.sum(jnp.where(match, places[None, :], 0), axis=1)
    live_slot = jnp.any(match, axis=1)
    return channel_of, live_slot


def gram_kernel(scale, live_ref, data_ref, out_ref):
    live = live_ref[pl.program_id(0)] > 0

    @pl.when(jnp.logical_not(live))
    def _():
        out_ref[...] = jnp.zeros_like(out_ref)

    @pl.when(live)
    def _():
        multiply_slot(scale, data_ref, out_ref)


def multiply_slot(scale, data_ref, out_ref):
    inps, chans, _, _, frames, width = data_ref.shape
    parts = []
    for part in range(2):
        blocks = [
            data_ref[z, :, 0, part].reshape(chans * frames, width) for z in range(inps)
        ]
        parts.append(jnp.concatenate(blocks, axis=1))
    real, imag = parts
    both = jnp.concatenate([real, imag], axis=0)
    turned = jnp.concatenate([imag, -real], axis=0)
    tile = out_ref.shape[2]
    for lhs, part in ((both, 0), (turned, 1)):
        for row in range(0, tile, 256):
            out_ref[0, part, row : row + 256] = (
                lax.dot_general(
                    lhs[:, row : row + 256],
                    both,
                    (((0,), (0,)), ((), ())),
                    preferred_element_type=jnp.float32,
                )
                * scale
            )


def correlate(live, arrived, frames_total):
    inps, chans, slots, _, frames, width = arrived.shape
    total = inps * width
    return pl.pallas_call(
        functools.partial(gram_kernel, 1.0 / frames_total),
        grid_spec=pltpu.PrefetchScalarGridSpec(
            num_scalar_prefetch=1,
            grid=(slots,),
            in_specs=[
                pl.BlockSpec((inps, chans, 1, 2, frames, width), lambda s, live: (0, 0, s, 0, 0, 0))
            ],
            out_specs=pl.BlockSpec((1, 2, total, total), lambda s, live: (s, 0, 0, 0)),
        ),
        out_shape=jax.ShapeDtypeStruct((slots, 2, total, total), jnp.float32),
        compiler_params=pltpu.CompilerParams(vmem_limit_bytes=VMEM_BYTES),
        cost_estimate=pl.CostEstimate(
            flops=slots * 2 * 2 * total * total * 2 * chans * frames,
            bytes_accessed=slots * 2 * total * total * 4,
            transcendentals=0,
        ),
    )(live, arrived)


SIN_TERMS = [
    (-1) ** n * (2 * math.pi) ** (2 * n + 1) / math.factorial(2 * n + 1) for n in range(9)
]
COS_TERMS = [(-1) ** n * (2 * math.pi) ** (2 * n) / math.factorial(2 * n) for n in range(10)]


def turn_pair(turns):
    rest = turns - jnp.round(turns)
    square = rest * rest
    sine = jnp.full_like(square, SIN_TERMS[-1])
    for term in SIN_TERMS[-2::-1]:
        sine = sine * square + term
    cosine = jnp.full_like(square, COS_TERMS[-1])
    for term in COS_TERMS[-2::-1]:
        cosine = cosine * square + term
    return cosine, sine * rest


MESH = pl.DeviceIdType.MESH
GROUP = 4


def exchange_kernel(
    length_total,
    inverse,
    mine,
    outgoing,
    delay_ref,
    arrived,
    formed,
    data,
    middle,
    part,
    leaving,
    up,
    down,
    state,
    step,
    data_send,
    data_recv,
    cross_send,
    cross_recv,
    deal_send,
    deal_recv,
    up_send,
    up_recv,
    down_send,
    down_recv,
    own_sem,
):
    inps = lax.axis_size("inp")
    chans = lax.axis_size("chan")
    z = lax.axis_index("inp")
    me = lax.axis_index("chan")
    _, held, _, frames, width = mine.shape
    groups = held // GROUP
    beams = delay_ref.shape[1]
    span = beams // inps
    half = chans * frames

    barrier = pltpu.get_barrier_semaphore()
    for r in range(1, inps):
        pl.semaphore_signal(
            barrier, inc=1, device_id=(lax.rem(z + r, inps), me), device_id_type=MESH
        )

    @pl.loop(1, chans)
    def _(q):
        pl.semaphore_signal(
            barrier, inc=1, device_id=(z, lax.rem(me + q, chans)), device_id_type=MESH
        )

    pl.semaphore_wait(barrier, inps + chans - 2)

    def rows_of(g):
        return pl.ds(g * GROUP, GROUP)

    def data_copy(g, q):
        peer = lax.rem(me + q, chans)
        return pltpu.make_async_remote_copy(
            src_ref=mine.at[peer, rows_of(g)],
            dst_ref=data.at[me, rows_of(g)],
            send_sem=data_send.at[g, q],
            recv_sem=data_recv.at[g, q],
            device_id=(z, peer),
            device_id_type=MESH,
        )

    def cross_copy(r):
        peer = lax.rem(z + r, inps)
        return pltpu.make_async_remote_copy(
            src_ref=outgoing.at[peer],
            dst_ref=middle.at[r],
            send_sem=cross_send.at[r],
            recv_sem=cross_recv.at[r],
            device_id=(peer, me),
            device_id_type=MESH,
        )

    def deal_block(r):
        return outgoing.at[z] if r == 0 else middle.at[r]

    def deal_copy(r, q):
        peer = lax.rem(me + q, chans)
        return pltpu.make_async_remote_copy(
            src_ref=deal_block(r).at[peer],
            dst_ref=arrived.at[lax.rem(z + inps - r, inps), me],
            send_sem=deal_send.at[r, q],
            recv_sem=deal_recv.at[r, q],
            device_id=(z, peer),
            device_id_type=MESH,
        )

    def deal_own(r):
        return pltpu.make_async_copy(
            deal_block(r).at[me],
            arrived.at[lax.rem(z + inps - r, inps), me],
            own_sem.at[r],
        )

    def up_copy(d, g):
        return pltpu.make_async_remote_copy(
            src_ref=leaving.at[d, rows_of(g)],
            dst_ref=up.at[d, rows_of(g)],
            send_sem=up_send.at[d, g],
            recv_sem=up_recv.at[d, g],
            device_id=(lax.rem(z + 1, inps), me),
            device_id_type=MESH,
        )

    def down_copy(d, g):
        return pltpu.make_async_remote_copy(
            src_ref=leaving.at[d, rows_of(g)],
            dst_ref=down.at[d, rows_of(g)],
            send_sem=down_send.at[d, g],
            recv_sem=down_recv.at[d, g],
            device_id=(lax.rem(z + inps - 1, inps), me),
            device_id_type=MESH,
        )

    own_data = pltpu.make_async_copy(mine.at[me], data.at[me], own_sem.at[inps])
    own_data.start()

    @pl.loop(1, chans)
    def _(q):
        data_copy(0, q).start()

    for r in range(1, inps):
        cross_copy(r).start()

    @pl.loop(1, groups)
    def _(g):
        @pl.loop(1, chans)
        def _(q):
            data_copy(g, q).start()

    def deal(r):
        deal_own(r).start()

        @pl.loop(1, chans)
        def _(q):
            deal_copy(r, q).start()

    deal(0)

    first = (me * held).astype(jnp.float32)

    @pl.loop(0, width // 32)
    def _(block):
        rows = pl.ds(pl.multiple_of(block * 32, 32), 32)
        delay = delay_ref[rows]
        cosine, sine = turn_pair(delay * (1.0 / length_total))
        step[0, rows] = cosine
        step[1, rows] = -sine
        cosine, sine = turn_pair((first * delay) * (1.0 / length_total))
        state[0, rows] = cosine * inverse
        state[1, rows] = -sine * inverse

    own_data.wait()

    def compute(g):
        @pl.loop(1, chans)
        def _(q):
            data_copy(g, q).wait_recv()

        @pl.loop(0, GROUP)
        def _(offset):
            c = g * GROUP + offset
            real_state = state[0]
            imag_state = state[1]
            real_weight = real_state.astype(jnp.bfloat16)
            imag_weight = imag_state.astype(jnp.bfloat16)
            real_step = step[0]
            imag_step = step[1]
            state[0] = real_state * real_step - imag_state * imag_step
            state[1] = real_state * imag_step + imag_state * real_step
            both = jnp.concatenate(
                [data[:, c, 0].reshape(half, width), data[:, c, 1].reshape(half, width)], axis=0
            )
            by_real = jnp.dot(both, real_weight, preferred_element_type=jnp.float32)
            by_imag = jnp.dot(both, imag_weight, preferred_element_type=jnp.float32)
            real_beam = by_real[:half] - by_imag[half:]
            imag_beam = by_real[half:] + by_imag[:half]
            for d in range(inps):
                cols = slice(d * span, (d + 1) * span)
                part[d, c] = jnp.concatenate([real_beam[:, cols], imag_beam[:, cols]], axis=1)

    def relay(g):
        rows = rows_of(g)
        for d in range(inps - 1, 0, -1):

            @pl.when(z < d)
            def _():
                @pl.when(z == 0)
                def _():
                    leaving[d, rows] = part[d, rows].astype(jnp.bfloat16)

                @pl.when(z > 0)
                def _():
                    up_copy(d, g).wait_recv()
                    leaving[d, rows] = (
                        part[d, rows] + up[d, rows].astype(jnp.float32)
                    ).astype(jnp.bfloat16)

                up_copy(d, g).start()

        for d in range(inps - 1):

            @pl.when(z > d)
            def _():
                @pl.when(z == inps - 1)
                def _():
                    leaving[d, rows] = part[d, rows].astype(jnp.bfloat16)

                @pl.when(z < inps - 1)
                def _():
                    down_copy(d, g).wait_recv()
                    leaving[d, rows] = (
                        part[d, rows] + down[d, rows].astype(jnp.float32)
                    ).astype(jnp.bfloat16)

                down_copy(d, g).start()

        for d in range(inps):

            @pl.when(z == d)
            def _():
                total = part[d, rows]
                if d > 0:
                    up_copy(d, g).wait_recv()
                    total = total + up[d, rows].astype(jnp.float32)
                if d < inps - 1:
                    down_copy(d, g).wait_recv()
                    total = total + down[d, rows].astype(jnp.float32)
                formed[rows] = total.astype(jnp.bfloat16)

    compute(0)

    @pl.loop(1, groups)
    def _(g):
        compute(g)
        relay(g - 1)

    def forward(r):
        cross_copy(r).wait_recv()
        deal(r)

    for r in range(1, inps):
        forward(r)
    relay(groups - 1)

    for r in range(1, inps):
        cross_copy(r).wait_send()
    for r in range(inps):
        deal_own(r).wait()

        @pl.loop(1, chans)
        def _(q):
            deal_copy(r, q).wait()

    @pl.loop(0, groups)
    def _(g):
        @pl.loop(1, chans)
        def _(q):
            data_copy(g, q).wait_send()

        for d in range(1, inps):

            @pl.when(z < d)
            def _():
                up_copy(d, g).wait_send()

        for d in range(inps - 1):

            @pl.when(z > d)
            def _():
                down_copy(d, g).wait_send()


def exchange(mine, outgoing, delays, length_total, all_inputs):
    inps = outgoing.shape[0]
    chans, held, _, frames, width = mine.shape
    beams = delays.shape[1]
    groups = held // GROUP
    formed_shape = (held, chans * frames, 2 * beams // inps)
    dma = pltpu.SemaphoreType.DMA
    return pl.pallas_call(
        functools.partial(exchange_kernel, length_total, 1.0 / math.sqrt(all_inputs)),
        in_specs=[
            pl.BlockSpec(memory_space=pl.ANY),
            pl.BlockSpec(memory_space=pl.ANY),
            pl.BlockSpec(memory_space=pltpu.VMEM),
        ],
        out_specs=[
            pl.BlockSpec(memory_space=pl.ANY),
            pl.BlockSpec(memory_space=pltpu.VMEM),
        ],
        out_shape=[
            jax.ShapeDtypeStruct(outgoing.shape, jnp.bfloat16),
            jax.ShapeDtypeStruct(formed_shape, jnp.bfloat16),
        ],
        scratch_shapes=[
            pltpu.VMEM(mine.shape, jnp.bfloat16),
            pltpu.VMEM(outgoing.shape, jnp.bfloat16),
            pltpu.VMEM((inps, *formed_shape), jnp.float32),
            pltpu.VMEM((inps, *formed_shape), jnp.bfloat16),
            pltpu.VMEM((inps, *formed_shape), jnp.bfloat16),
            pltpu.VMEM((inps, *formed_shape), jnp.bfloat16),
            pltpu.VMEM((2, width, beams), jnp.float32),
            pltpu.VMEM((2, width, beams), jnp.float32),
            dma((groups, chans)),
            dma((groups, chans)),
            dma((inps,)),
            dma((inps,)),
            dma((inps, chans)),
            dma((inps, chans)),
            dma((inps, groups)),
            dma((inps, groups)),
            dma((inps, groups)),
            dma((inps, groups)),
            dma((inps + 1,)),
        ],
        compiler_params=pltpu.CompilerParams(
            collective_id=0, has_side_effects=True, vmem_limit_bytes=VMEM_BYTES
        ),
        cost_estimate=pl.CostEstimate(
            flops=held * 2 * 4 * chans * frames * width * beams,
            bytes_accessed=held * chans * frames * (4 * width + 4 * beams),
            transcendentals=0,
        ),
    )(mine, outgoing, delays)


def shards(samples, gram_owner, beam_owner, delays, sections):
    input_count, frame_count, length_total = samples.shape
    half_count = length_total // 2
    inp_count = lax.axis_size("inp")
    chan_count = lax.axis_size("chan")
    inp_here = lax.axis_index("inp")
    chan_here = lax.axis_index("chan")
    all_inputs = input_count * inp_count
    all_frames = frame_count * chan_count
    owner_count = inp_count * chan_count
    gram_slots = 2 * gram_owner.shape[0] // owner_count
    beam_slots = 2 * half_count // chan_count
    held = half_count // chan_count
    table = fourier_table(length_total)
    spectra = jnp.einsum(
        "kpw,ifw->kpfi", table, samples, preferred_element_type=jnp.float32
    ).astype(jnp.bfloat16)

    mine = spectra.reshape(chan_count, held, 2, frame_count, input_count)
    gram_channel, gram_live = slot_table(gram_owner, owner_count, gram_slots)
    outgoing = jnp.take(spectra, gram_channel, axis=0).reshape(
        inp_count, chan_count, gram_slots, 2, frame_count, input_count
    )
    gram_live = gram_live.astype(jnp.int32).reshape(owner_count, gram_slots)
    gram_live = lax.dynamic_index_in_dim(gram_live, inp_here * chan_count + chan_here, 0, False)

    delay_cols = lax.dynamic_slice_in_dim(delays, inp_here * input_count, input_count, 1)
    ordered = jnp.take(delay_cols, sections, axis=0).T
    arrived, formed = exchange(mine, outgoing, ordered, length_total, all_inputs)
    every = lax.all_gather(formed, "chan", axis=0, tiled=True)

    visibilities = correlate(gram_live, arrived, all_frames)

    beam_channel, beam_live = slot_table(beam_owner, chan_count, beam_slots)
    here = lax.dynamic_slice_in_dim(beam_channel, chan_here * beam_slots, beam_slots)
    live = lax.dynamic_slice_in_dim(beam_live, chan_here * beam_slots, beam_slots)
    voltages = jnp.where(
        live[:, None, None], jnp.take(every, here, axis=0), jnp.zeros((), jnp.bfloat16)
    ).astype(jnp.float32)
    return (visibilities, voltages[:, None])


def solution(mesh):
    return jax.shard_map(
        shards,
        mesh=mesh,
        in_specs=(P("inp", "chan", None), P(), P(), P(), P()),
        out_specs=(P(("inp", "chan"), None, None, None), P("chan", "inp", None, None)),
        check_vma=False,
    )
```

```python
import functools
import math

import jax
import jax.numpy as jnp
import numpy as np
from jax import lax
from jax.experimental import pallas as pl
from jax.experimental.pallas import tpu as pltpu
from jax.sharding import PartitionSpec as P

VMEM_BYTES = 56 * 1024 * 1024


def fourier_table(length_total):
    half_count = length_total // 2
    rows = np.arange(half_count, dtype=np.int32)
    cols = np.arange(length_total, dtype=np.int32)
    turns = (rows[:, None] * cols[None, :] % length_total).astype(np.float32) * np.float32(
        2.0 * math.pi / length_total
    )
    factor = np.float32(1.0 / math.sqrt(length_total))
    table = np.stack([np.cos(turns) * factor, -np.sin(turns) * factor], axis=1)
    return jnp.asarray(table.astype(jnp.bfloat16))


def slot_table(owner_list, owner_count, slot_count):
    count = owner_list.shape[0]
    places = jnp.arange(count, dtype=jnp.int32)
    before = (owner_list[None, :] == owner_list[:, None]) & (places[None, :] < places[:, None])
    slot_of = jnp.sum(before.astype(jnp.int32), axis=1)
    keys = owner_list * slot_count + slot_of
    targets = jnp.arange(owner_count * slot_count, dtype=jnp.int32)
    match = keys[None, :] == targets[:, None]
    channel_of = jnp.sum(jnp.where(match, places[None, :], 0), axis=1)
    live_slot = jnp.any(match, axis=1)
    return channel_of, live_slot


def gram_kernel(scale, live_ref, data_ref, out_ref):
    live = live_ref[pl.program_id(0)] > 0

    @pl.when(jnp.logical_not(live))
    def _():
        out_ref[...] = jnp.zeros_like(out_ref)

    @pl.when(live)
    def _():
        multiply_slot(scale, data_ref, out_ref)


def multiply_slot(scale, data_ref, out_ref):
    inps, chans, _, _, frames, width = data_ref.shape
    parts = []
    for part in range(2):
        blocks = [
            data_ref[z, :, 0, part].reshape(chans * frames, width) for z in range(inps)
        ]
        parts.append(jnp.concatenate(blocks, axis=1))
    real, imag = parts
    both = jnp.concatenate([real, imag], axis=0)
    turned = jnp.concatenate([imag, -real], axis=0)
    tile = out_ref.shape[2]
    for lhs, part in ((both, 0), (turned, 1)):
        for row in range(0, tile, 256):
            out_ref[0, part, row : row + 256] = (
                lax.dot_general(
                    lhs[:, row : row + 256],
                    both,
                    (((0,), (0,)), ((), ())),
                    preferred_element_type=jnp.float32,
                )
                * scale
            )


def correlate(live, arrived, frames_total):
    inps, chans, slots, _, frames, width = arrived.shape
    total = inps * width
    return pl.pallas_call(
        functools.partial(gram_kernel, 1.0 / frames_total),
        grid_spec=pltpu.PrefetchScalarGridSpec(
            num_scalar_prefetch=1,
            grid=(slots,),
            in_specs=[
                pl.BlockSpec((inps, chans, 1, 2, frames, width), lambda s, live: (0, 0, s, 0, 0, 0))
            ],
            out_specs=pl.BlockSpec((1, 2, total, total), lambda s, live: (s, 0, 0, 0)),
        ),
        out_shape=jax.ShapeDtypeStruct((slots, 2, total, total), jnp.float32),
        compiler_params=pltpu.CompilerParams(vmem_limit_bytes=VMEM_BYTES),
        cost_estimate=pl.CostEstimate(
            flops=slots * 2 * 2 * total * total * 2 * chans * frames,
            bytes_accessed=slots * 2 * total * total * 4,
            transcendentals=0,
        ),
    )(live, arrived)


SIN_TERMS = [
    (-1) ** n * (2 * math.pi) ** (2 * n + 1) / math.factorial(2 * n + 1) for n in range(9)
]
COS_TERMS = [(-1) ** n * (2 * math.pi) ** (2 * n) / math.factorial(2 * n) for n in range(10)]


def turn_pair(turns):
    rest = turns - jnp.round(turns)
    square = rest * rest
    sine = jnp.full_like(square, SIN_TERMS[-1])
    for term in SIN_TERMS[-2::-1]:
        sine = sine * square + term
    cosine = jnp.full_like(square, COS_TERMS[-1])
    for term in COS_TERMS[-2::-1]:
        cosine = cosine * square + term
    return cosine, sine * rest


MESH = pl.DeviceIdType.MESH
GROUP = 4


def exchange_kernel(
    length_total,
    inverse,
    mine,
    outgoing,
    delay_ref,
    arrived,
    formed,
    data,
    middle,
    part,
    leaving,
    up,
    down,
    state,
    step,
    data_send,
    data_recv,
    cross_send,
    cross_recv,
    deal_send,
    deal_recv,
    up_send,
    up_recv,
    down_send,
    down_recv,
    own_sem,
):
    inps = lax.axis_size("inp")
    chans = lax.axis_size("chan")
    z = lax.axis_index("inp")
    me = lax.axis_index("chan")
    _, held, _, frames, width = mine.shape
    groups = held // GROUP
    beams = delay_ref.shape[1]
    span = beams // inps
    half = chans * frames

    barrier = pltpu.get_barrier_semaphore()
    for r in range(1, inps):
        pl.semaphore_signal(
            barrier, inc=1, device_id=(lax.rem(z + r, inps), me), device_id_type=MESH
        )

    @pl.loop(1, chans)
    def _(q):
        pl.semaphore_signal(
            barrier, inc=1, device_id=(z, lax.rem(me + q, chans)), device_id_type=MESH
        )

    pl.semaphore_wait(barrier, inps + chans - 2)

    def rows_of(g):
        return pl.ds(g * GROUP, GROUP)

    def data_copy(g, q):
        peer = lax.rem(me + q, chans)
        return pltpu.make_async_remote_copy(
            src_ref=mine.at[peer, rows_of(g)],
            dst_ref=data.at[me, rows_of(g)],
            send_sem=data_send.at[g, q],
            recv_sem=data_recv.at[g, q],
            device_id=(z, peer),
            device_id_type=MESH,
        )

    def cross_copy(r, q):
        peer = lax.rem(z + r, inps)
        target = lax.rem(me + q, chans)
        return pltpu.make_async_remote_copy(
            src_ref=outgoing.at[peer, target],
            dst_ref=middle.at[r, target],
            send_sem=cross_send.at[r, q],
            recv_sem=cross_recv.at[r, q],
            device_id=(peer, me),
            device_id_type=MESH,
        )

    def deal_block(r):
        return outgoing.at[z] if r == 0 else middle.at[r]

    def deal_copy(r, q):
        peer = lax.rem(me + q, chans)
        return pltpu.make_async_remote_copy(
            src_ref=deal_block(r).at[peer],
            dst_ref=arrived.at[lax.rem(z + inps - r, inps), me],
            send_sem=deal_send.at[r, q],
            recv_sem=deal_recv.at[r, q],
            device_id=(z, peer),
            device_id_type=MESH,
        )

    def deal_own(r):
        return pltpu.make_async_copy(
            deal_block(r).at[me],
            arrived.at[lax.rem(z + inps - r, inps), me],
            own_sem.at[r],
        )

    def up_copy(d, g):
        return pltpu.make_async_remote_copy(
            src_ref=leaving.at[d, rows_of(g)],
            dst_ref=up.at[d, rows_of(g)],
            send_sem=up_send.at[d, g],
            recv_sem=up_recv.at[d, g],
            device_id=(lax.rem(z + 1, inps), me),
            device_id_type=MESH,
        )

    def down_copy(d, g):
        return pltpu.make_async_remote_copy(
            src_ref=leaving.at[d, rows_of(g)],
            dst_ref=down.at[d, rows_of(g)],
            send_sem=down_send.at[d, g],
            recv_sem=down_recv.at[d, g],
            device_id=(lax.rem(z + inps - 1, inps), me),
            device_id_type=MESH,
        )

    own_data = pltpu.make_async_copy(mine.at[me], data.at[me], own_sem.at[inps])
    own_data.start()
    share = chans // groups

    def send_data(g):
        @pl.loop(1, chans)
        def _(q):
            data_copy(g, q).start()

    def send_cross(g):
        @pl.loop(g * share, (g + 1) * share)
        def _(q):
            for r in range(1, inps):
                cross_copy(r, q).start()

    def deal_on(g):
        @pl.loop(g * share, (g + 1) * share)
        def _(q):
            for r in range(1, inps):
                cross_copy(r, q).wait_recv()

            @pl.when(q == 0)
            def _():
                for r in range(inps):
                    deal_own(r).start()

            @pl.when(q > 0)
            def _():
                for r in range(inps):
                    deal_copy(r, q).start()

    send_data(0)
    send_cross(0)
    send_data(1)

    first = (me * held).astype(jnp.float32)

    @pl.loop(0, width // 32)
    def _(block):
        rows = pl.ds(pl.multiple_of(block * 32, 32), 32)
        delay = delay_ref[rows]
        cosine, sine = turn_pair(delay * (1.0 / length_total))
        step[0, rows] = cosine
        step[1, rows] = -sine
        cosine, sine = turn_pair((first * delay) * (1.0 / length_total))
        state[0, rows] = cosine * inverse
        state[1, rows] = -sine * inverse

    own_data.wait()

    def compute(g):
        @pl.loop(1, chans)
        def _(q):
            data_copy(g, q).wait_recv()

        @pl.loop(0, GROUP)
        def _(offset):
            c = g * GROUP + offset
            real_state = state[0]
            imag_state = state[1]
            real_weight = real_state.astype(jnp.bfloat16)
            imag_weight = imag_state.astype(jnp.bfloat16)
            real_step = step[0]
            imag_step = step[1]
            state[0] = real_state * real_step - imag_state * imag_step
            state[1] = real_state * imag_step + imag_state * real_step
            both = jnp.concatenate(
                [data[:, c, 0].reshape(half, width), data[:, c, 1].reshape(half, width)], axis=0
            )
            by_real = jnp.dot(both, real_weight, preferred_element_type=jnp.float32)
            by_imag = jnp.dot(both, imag_weight, preferred_element_type=jnp.float32)
            real_beam = by_real[:half] - by_imag[half:]
            imag_beam = by_real[half:] + by_imag[:half]
            for d in range(inps):
                cols = slice(d * span, (d + 1) * span)
                part[d, c] = jnp.concatenate([real_beam[:, cols], imag_beam[:, cols]], axis=1)

    def pass_up(g):
        rows = rows_of(g)
        for d in range(inps - 1, 0, -1):

            @pl.when(z < d)
            def _():
                @pl.when(z == 0)
                def _():
                    leaving[d, rows] = part[d, rows].astype(jnp.bfloat16)

                @pl.when(z > 0)
                def _():
                    up_copy(d, g).wait_recv()
                    leaving[d, rows] = (
                        part[d, rows] + up[d, rows].astype(jnp.float32)
                    ).astype(jnp.bfloat16)

                up_copy(d, g).start()

    def pass_down(g):
        rows = rows_of(g)
        for d in range(inps - 1):

            @pl.when(z > d)
            def _():
                @pl.when(z == inps - 1)
                def _():
                    leaving[d, rows] = part[d, rows].astype(jnp.bfloat16)

                @pl.when(z < inps - 1)
                def _():
                    down_copy(d, g).wait_recv()
                    leaving[d, rows] = (
                        part[d, rows] + down[d, rows].astype(jnp.float32)
                    ).astype(jnp.bfloat16)

                down_copy(d, g).start()

    def finish(g):
        rows = rows_of(g)
        for d in range(inps):

            @pl.when(z == d)
            def _():
                total = part[d, rows]
                if d > 0:
                    up_copy(d, g).wait_recv()
                    total = total + up[d, rows].astype(jnp.float32)
                if d < inps - 1:
                    down_copy(d, g).wait_recv()
                    total = total + down[d, rows].astype(jnp.float32)
                formed[rows] = total.astype(jnp.bfloat16)

    @pl.loop(0, groups + inps)
    def _(turn):
        @pl.when(turn + 2 < groups)
        def _():
            send_data(turn + 2)

        @pl.when(turn < groups)
        def _():
            compute(turn)

        up_group = turn - z

        @pl.when((up_group >= 0) & (up_group < groups))
        def _():
            pass_up(up_group)

        down_group = turn - (inps - 1 - z)

        @pl.when((down_group >= 0) & (down_group < groups))
        def _():
            pass_down(down_group)

        @pl.when(turn + 1 < groups)
        def _():
            send_cross(turn + 1)

        @pl.when((turn >= 2) & (turn - 2 < groups))
        def _():
            deal_on(turn - 2)

        @pl.when(turn >= inps)
        def _():
            finish(turn - inps)

    @pl.loop(0, chans)
    def _(q):
        for r in range(1, inps):
            cross_copy(r, q).wait_send()

    for r in range(inps):
        deal_own(r).wait()

        @pl.loop(1, chans)
        def _(q):
            deal_copy(r, q).wait()

    @pl.loop(0, groups)
    def _(g):
        @pl.loop(1, chans)
        def _(q):
            data_copy(g, q).wait_send()

        for d in range(1, inps):

            @pl.when(z < d)
            def _():
                up_copy(d, g).wait_send()

        for d in range(inps - 1):

            @pl.when(z > d)
            def _():
                down_copy(d, g).wait_send()


def exchange(mine, outgoing, delays, length_total, all_inputs):
    inps = outgoing.shape[0]
    chans, held, _, frames, width = mine.shape
    beams = delays.shape[1]
    groups = held // GROUP
    formed_shape = (held, chans * frames, 2 * beams // inps)
    dma = pltpu.SemaphoreType.DMA
    return pl.pallas_call(
        functools.partial(exchange_kernel, length_total, 1.0 / math.sqrt(all_inputs)),
        in_specs=[
            pl.BlockSpec(memory_space=pl.ANY),
            pl.BlockSpec(memory_space=pl.ANY),
            pl.BlockSpec(memory_space=pltpu.VMEM),
        ],
        out_specs=[
            pl.BlockSpec(memory_space=pl.ANY),
            pl.BlockSpec(memory_space=pltpu.VMEM),
        ],
        out_shape=[
            jax.ShapeDtypeStruct(outgoing.shape, jnp.bfloat16),
            jax.ShapeDtypeStruct(formed_shape, jnp.bfloat16),
        ],
        scratch_shapes=[
            pltpu.VMEM(mine.shape, jnp.bfloat16),
            pltpu.VMEM(outgoing.shape, jnp.bfloat16),
            pltpu.VMEM((inps, *formed_shape), jnp.float32),
            pltpu.VMEM((inps, *formed_shape), jnp.bfloat16),
            pltpu.VMEM((inps, *formed_shape), jnp.bfloat16),
            pltpu.VMEM((inps, *formed_shape), jnp.bfloat16),
            pltpu.VMEM((2, width, beams), jnp.float32),
            pltpu.VMEM((2, width, beams), jnp.float32),
            dma((groups, chans)),
            dma((groups, chans)),
            dma((inps, chans)),
            dma((inps, chans)),
            dma((inps, chans)),
            dma((inps, chans)),
            dma((inps, groups)),
            dma((inps, groups)),
            dma((inps, groups)),
            dma((inps, groups)),
            dma((inps + 1,)),
        ],
        compiler_params=pltpu.CompilerParams(
            collective_id=0, has_side_effects=True, vmem_limit_bytes=VMEM_BYTES
        ),
        cost_estimate=pl.CostEstimate(
            flops=held * 2 * 4 * chans * frames * width * beams,
            bytes_accessed=held * chans * frames * (4 * width + 4 * beams),
            transcendentals=0,
        ),
    )(mine, outgoing, delays)


def shards(samples, gram_owner, beam_owner, delays, sections):
    input_count, frame_count, length_total = samples.shape
    half_count = length_total // 2
    inp_count = lax.axis_size("inp")
    chan_count = lax.axis_size("chan")
    inp_here = lax.axis_index("inp")
    chan_here = lax.axis_index("chan")
    all_inputs = input_count * inp_count
    all_frames = frame_count * chan_count
    owner_count = inp_count * chan_count
    gram_slots = 2 * gram_owner.shape[0] // owner_count
    beam_slots = 2 * half_count // chan_count
    held = half_count // chan_count
    table = fourier_table(length_total)
    spectra = jnp.einsum(
        "kpw,ifw->kpfi", table, samples, preferred_element_type=jnp.float32
    ).astype(jnp.bfloat16)

    mine = spectra.reshape(chan_count, held, 2, frame_count, input_count)
    gram_channel, gram_live = slot_table(gram_owner, owner_count, gram_slots)
    outgoing = jnp.take(spectra, gram_channel, axis=0, mode="clip").reshape(
        inp_count, chan_count, gram_slots, 2, frame_count, input_count
    )
    gram_live = gram_live.astype(jnp.int32).reshape(owner_count, gram_slots)
    gram_live = lax.dynamic_index_in_dim(gram_live, inp_here * chan_count + chan_here, 0, False)

    delay_cols = lax.dynamic_slice_in_dim(delays, inp_here * input_count, input_count, 1)
    ordered = jnp.take(delay_cols, sections, axis=0, mode="clip").T
    arrived, formed = exchange(mine, outgoing, ordered, length_total, all_inputs)
    every = lax.all_gather(formed, "chan", axis=0, tiled=True)

    visibilities = correlate(gram_live, arrived, all_frames)

    beam_channel, beam_live = slot_table(beam_owner, chan_count, beam_slots)
    here = lax.dynamic_slice_in_dim(beam_channel, chan_here * beam_slots, beam_slots)
    live = lax.dynamic_slice_in_dim(beam_live, chan_here * beam_slots, beam_slots)
    voltages = jnp.where(
        live[:, None, None], jnp.take(every, here, axis=0, mode="clip"), jnp.zeros((), jnp.bfloat16)
    ).astype(jnp.float32)
    return (visibilities, voltages[:, None])


def solution(mesh):
    return jax.shard_map(
        shards,
        mesh=mesh,
        in_specs=(P("inp", "chan", None), P(), P(), P(), P()),
        out_specs=(P(("inp", "chan"), None, None, None), P("chan", "inp", None, None)),
        check_vma=False,
    )
```

```python
import functools
import math

import jax
import jax.numpy as jnp
import numpy as np
from jax import lax
from jax.experimental import pallas as pl
from jax.experimental.pallas import tpu as pltpu
from jax.sharding import PartitionSpec as P

VMEM_BYTES = 56 * 1024 * 1024


def fourier_table(length_total):
    half_count = length_total // 2
    rows = np.arange(half_count, dtype=np.int32)
    cols = np.arange(length_total, dtype=np.int32)
    turns = (rows[:, None] * cols[None, :] % length_total).astype(np.float32) * np.float32(
        2.0 * math.pi / length_total
    )
    factor = np.float32(1.0 / math.sqrt(length_total))
    table = np.stack([np.cos(turns) * factor, -np.sin(turns) * factor], axis=1)
    return jnp.asarray(table.astype(jnp.bfloat16))


def slot_table(owner_list, owner_count, slot_count):
    count = owner_list.shape[0]
    places = jnp.arange(count, dtype=jnp.int32)
    before = (owner_list[None, :] == owner_list[:, None]) & (places[None, :] < places[:, None])
    slot_of = jnp.sum(before.astype(jnp.int32), axis=1)
    keys = owner_list * slot_count + slot_of
    targets = jnp.arange(owner_count * slot_count, dtype=jnp.int32)
    match = keys[None, :] == targets[:, None]
    channel_of = jnp.sum(jnp.where(match, places[None, :], 0), axis=1)
    live_slot = jnp.any(match, axis=1)
    return channel_of, live_slot


def gram_kernel(
    scale, per_step, live_ref, here_ref, beam_live_ref, data_ref, *refs
):
    beam_refs = refs[:per_step]
    out_ref, volt_ref = refs[per_step:]
    slot = pl.program_id(0)
    for j, beam_ref in enumerate(beam_refs):
        alive = beam_live_ref[slot * per_step + j] > 0
        volt_ref[j] = jnp.where(alive, beam_ref[0].astype(jnp.float32), 0.0)

    live = live_ref[slot] > 0

    @pl.when(jnp.logical_not(live))
    def _():
        out_ref[...] = jnp.zeros_like(out_ref)

    @pl.when(live)
    def _():
        multiply_slot(scale, data_ref, out_ref)


def multiply_slot(scale, data_ref, out_ref):
    inps, chans, _, _, frames, width = data_ref.shape
    parts = []
    for part in range(2):
        blocks = [
            data_ref[z, :, 0, part].reshape(chans * frames, width) for z in range(inps)
        ]
        parts.append(jnp.concatenate(blocks, axis=1))
    real, imag = parts
    both = jnp.concatenate([real, imag], axis=0)
    turned = jnp.concatenate([imag, -real], axis=0)
    tile = out_ref.shape[2]
    for lhs, part in ((both, 0), (turned, 1)):
        for row in range(0, tile, 256):
            out_ref[0, part, row : row + 256] = (
                lax.dot_general(
                    lhs[:, row : row + 256],
                    both,
                    (((0,), (0,)), ((), ())),
                    preferred_element_type=jnp.float32,
                )
                * scale
            )


def correlate(live, arrived, frames_total, here, beam_live, every):
    inps, chans, slots, _, frames, width = arrived.shape
    total = inps * width
    beam_slots = here.shape[0]
    per_step = beam_slots // slots
    rows, lanes = every.shape[1:]

    def beam_spec(j):
        return pl.BlockSpec(
            (1, rows, lanes), lambda s, live, here, beam_live: (here[s * per_step + j], 0, 0)
        )

    return pl.pallas_call(
        functools.partial(gram_kernel, 1.0 / frames_total, per_step),
        grid_spec=pltpu.PrefetchScalarGridSpec(
            num_scalar_prefetch=3,
            grid=(slots,),
            in_specs=[
                pl.BlockSpec((inps, chans, 1, 2, frames, width), lambda s, *_: (0, 0, s, 0, 0, 0)),
                *[beam_spec(j) for j in range(per_step)],
            ],
            out_specs=[
                pl.BlockSpec((1, 2, total, total), lambda s, *_: (s, 0, 0, 0)),
                pl.BlockSpec((per_step, rows, lanes), lambda s, *_: (s, 0, 0)),
            ],
        ),
        out_shape=[
            jax.ShapeDtypeStruct((slots, 2, total, total), jnp.float32),
            jax.ShapeDtypeStruct((beam_slots, rows, lanes), jnp.float32),
        ],
        compiler_params=pltpu.CompilerParams(vmem_limit_bytes=VMEM_BYTES),
        cost_estimate=pl.CostEstimate(
            flops=slots * 2 * 2 * total * total * 2 * chans * frames,
            bytes_accessed=slots * 2 * total * total * 4,
            transcendentals=0,
        ),
    )(live, here, beam_live, arrived, *[every] * per_step)


SIN_TERMS = [
    (-1) ** n * (2 * math.pi) ** (2 * n + 1) / math.factorial(2 * n + 1) for n in range(9)
]
COS_TERMS = [(-1) ** n * (2 * math.pi) ** (2 * n) / math.factorial(2 * n) for n in range(10)]


def turn_pair(turns):
    rest = turns - jnp.round(turns)
    square = rest * rest
    sine = jnp.full_like(square, SIN_TERMS[-1])
    for term in SIN_TERMS[-2::-1]:
        sine = sine * square + term
    cosine = jnp.full_like(square, COS_TERMS[-1])
    for term in COS_TERMS[-2::-1]:
        cosine = cosine * square + term
    return cosine, sine * rest


MESH = pl.DeviceIdType.MESH
GROUP = 4


def exchange_kernel(
    length_total,
    inverse,
    mine,
    outgoing,
    delay_ref,
    arrived,
    every,
    formed,
    data,
    middle,
    part,
    leaving,
    up,
    down,
    state,
    step,
    data_send,
    data_recv,
    cross_send,
    cross_recv,
    deal_send,
    deal_recv,
    up_send,
    up_recv,
    down_send,
    down_recv,
    own_sem,
    spread_send,
    spread_recv,
    hand_send,
    hand_recv,
    keep_sem,
):
    inps = lax.axis_size("inp")
    chans = lax.axis_size("chan")
    z = lax.axis_index("inp")
    me = lax.axis_index("chan")
    _, held, _, frames, width = mine.shape
    groups = held // GROUP
    beams = delay_ref.shape[1]
    span = beams // inps
    half = chans * frames

    barrier = pltpu.get_barrier_semaphore()
    for r in range(1, inps):
        pl.semaphore_signal(
            barrier, inc=1, device_id=(lax.rem(z + r, inps), me), device_id_type=MESH
        )

    @pl.loop(1, chans)
    def _(q):
        pl.semaphore_signal(
            barrier, inc=1, device_id=(z, lax.rem(me + q, chans)), device_id_type=MESH
        )

    pl.semaphore_wait(barrier, inps + chans - 2)

    def rows_of(g):
        return pl.ds(g * GROUP, GROUP)

    def data_copy(g, q):
        peer = lax.rem(me + q, chans)
        return pltpu.make_async_remote_copy(
            src_ref=mine.at[peer, rows_of(g)],
            dst_ref=data.at[me, rows_of(g)],
            send_sem=data_send.at[g, q],
            recv_sem=data_recv.at[g, q],
            device_id=(z, peer),
            device_id_type=MESH,
        )

    def cross_copy(r, q):
        peer = lax.rem(z + r, inps)
        target = lax.rem(me + q, chans)
        return pltpu.make_async_remote_copy(
            src_ref=outgoing.at[peer, target],
            dst_ref=middle.at[r, target],
            send_sem=cross_send.at[r, q],
            recv_sem=cross_recv.at[r, q],
            device_id=(peer, me),
            device_id_type=MESH,
        )

    def deal_block(r):
        return outgoing.at[z] if r == 0 else middle.at[r]

    def deal_copy(r, q):
        peer = lax.rem(me + q, chans)
        return pltpu.make_async_remote_copy(
            src_ref=deal_block(r).at[peer],
            dst_ref=arrived.at[lax.rem(z + inps - r, inps), me],
            send_sem=deal_send.at[r, q],
            recv_sem=deal_recv.at[r, q],
            device_id=(z, peer),
            device_id_type=MESH,
        )

    def deal_own(r):
        return pltpu.make_async_copy(
            deal_block(r).at[me],
            arrived.at[lax.rem(z + inps - r, inps), me],
            own_sem.at[r],
        )

    def up_copy(d, g):
        return pltpu.make_async_remote_copy(
            src_ref=leaving.at[d, rows_of(g)],
            dst_ref=up.at[d, rows_of(g)],
            send_sem=up_send.at[d, g],
            recv_sem=up_recv.at[d, g],
            device_id=(lax.rem(z + 1, inps), me),
            device_id_type=MESH,
        )

    def down_copy(d, g):
        return pltpu.make_async_remote_copy(
            src_ref=leaving.at[d, rows_of(g)],
            dst_ref=down.at[d, rows_of(g)],
            send_sem=down_send.at[d, g],
            recv_sem=down_recv.at[d, g],
            device_id=(lax.rem(z + inps - 1, inps), me),
            device_id_type=MESH,
        )

    sibling = me + 1 - 2 * lax.rem(me, 2)
    chips = chans // 2

    def spread_copy(p, g):
        peer = sibling if p is None else lax.rem(me + 2 * p, chans)
        slot = 0 if p is None else p
        return pltpu.make_async_remote_copy(
            src_ref=formed.at[rows_of(g)],
            dst_ref=every.at[me, rows_of(g)],
            send_sem=spread_send.at[slot, g],
            recv_sem=spread_recv.at[slot, g],
            device_id=(z, peer),
            device_id_type=MESH,
        )

    def hand_copy(p, g):
        source = lax.rem(me + chans - 2 * p, chans)
        return pltpu.make_async_remote_copy(
            src_ref=every.at[source, rows_of(g)],
            dst_ref=every.at[source, rows_of(g)],
            send_sem=hand_send.at[p, g],
            recv_sem=hand_recv.at[p, g],
            device_id=(z, sibling),
            device_id_type=MESH,
        )

    def keep_copy(g):
        return pltpu.make_async_copy(
            formed.at[rows_of(g)], every.at[me, rows_of(g)], keep_sem.at[g]
        )

    def spread(g):
        @pl.loop(1, chips)
        def _(p):
            spread_copy(p, g).start()

        spread_copy(None, g).start()
        keep_copy(g).start()

    def hand_on(g):
        @pl.loop(1, chips)
        def _(p):
            spread_copy(p, g).wait_recv()
            hand_copy(p, g).start()

    own_data = pltpu.make_async_copy(mine.at[me], data.at[me], own_sem.at[inps])
    own_data.start()
    share = chans // groups

    def send_data(g):
        @pl.loop(1, chans)
        def _(q):
            data_copy(g, q).start()

    def send_cross(g):
        @pl.loop(g * share, (g + 1) * share)
        def _(q):
            for r in range(1, inps):
                cross_copy(r, q).start()

    def deal_on(g):
        @pl.loop(g * share, (g + 1) * share)
        def _(q):
            for r in range(1, inps):
                cross_copy(r, q).wait_recv()

            @pl.when(q == 0)
            def _():
                for r in range(inps):
                    deal_own(r).start()

            @pl.when(q > 0)
            def _():
                for r in range(inps):
                    deal_copy(r, q).start()

    send_data(0)
    send_cross(0)
    send_data(1)

    first = (me * held).astype(jnp.float32)

    @pl.loop(0, width // 32)
    def _(block):
        rows = pl.ds(pl.multiple_of(block * 32, 32), 32)
        delay = delay_ref[rows]
        cosine, sine = turn_pair(delay * (1.0 / length_total))
        step[0, rows] = cosine
        step[1, rows] = -sine
        cosine, sine = turn_pair((first * delay) * (1.0 / length_total))
        state[0, rows] = cosine * inverse
        state[1, rows] = -sine * inverse

    own_data.wait()

    def compute(g):
        @pl.loop(1, chans)
        def _(q):
            data_copy(g, q).wait_recv()

        @pl.loop(0, GROUP)
        def _(offset):
            c = g * GROUP + offset
            real_state = state[0]
            imag_state = state[1]
            real_weight = real_state.astype(jnp.bfloat16)
            imag_weight = imag_state.astype(jnp.bfloat16)
            real_step = step[0]
            imag_step = step[1]
            state[0] = real_state * real_step - imag_state * imag_step
            state[1] = real_state * imag_step + imag_state * real_step
            both = jnp.concatenate(
                [data[:, c, 0].reshape(half, width), data[:, c, 1].reshape(half, width)], axis=0
            )
            by_real = jnp.dot(both, real_weight, preferred_element_type=jnp.float32)
            by_imag = jnp.dot(both, imag_weight, preferred_element_type=jnp.float32)
            real_beam = by_real[:half] - by_imag[half:]
            imag_beam = by_real[half:] + by_imag[:half]
            for d in range(inps):
                cols = slice(d * span, (d + 1) * span)
                part[d, c] = jnp.concatenate([real_beam[:, cols], imag_beam[:, cols]], axis=1)

    def pass_up(g):
        rows = rows_of(g)
        for d in range(inps - 1, 0, -1):

            @pl.when(z < d)
            def _():
                @pl.when(z == 0)
                def _():
                    leaving[d, rows] = part[d, rows].astype(jnp.bfloat16)

                @pl.when(z > 0)
                def _():
                    up_copy(d, g).wait_recv()
                    leaving[d, rows] = (
                        part[d, rows] + up[d, rows].astype(jnp.float32)
                    ).astype(jnp.bfloat16)

                up_copy(d, g).start()

    def pass_down(g):
        rows = rows_of(g)
        for d in range(inps - 1):

            @pl.when(z > d)
            def _():
                @pl.when(z == inps - 1)
                def _():
                    leaving[d, rows] = part[d, rows].astype(jnp.bfloat16)

                @pl.when(z < inps - 1)
                def _():
                    down_copy(d, g).wait_recv()
                    leaving[d, rows] = (
                        part[d, rows] + down[d, rows].astype(jnp.float32)
                    ).astype(jnp.bfloat16)

                down_copy(d, g).start()

    def finish(g):
        rows = rows_of(g)
        for d in range(inps):

            @pl.when(z == d)
            def _():
                total = part[d, rows]
                if d > 0:
                    up_copy(d, g).wait_recv()
                    total = total + up[d, rows].astype(jnp.float32)
                if d < inps - 1:
                    down_copy(d, g).wait_recv()
                    total = total + down[d, rows].astype(jnp.float32)
                formed[rows] = total.astype(jnp.bfloat16)

    @pl.loop(0, groups + inps + 2)
    def _(turn):
        @pl.when(turn + 2 < groups)
        def _():
            send_data(turn + 2)

        @pl.when(turn < groups)
        def _():
            compute(turn)

        up_group = turn - z

        @pl.when((up_group >= 0) & (up_group < groups))
        def _():
            pass_up(up_group)

        down_group = turn - (inps - 1 - z)

        @pl.when((down_group >= 0) & (down_group < groups))
        def _():
            pass_down(down_group)

        @pl.when(turn + 1 < groups)
        def _():
            send_cross(turn + 1)

        @pl.when((turn >= 2) & (turn - 2 < groups))
        def _():
            deal_on(turn - 2)

        @pl.when((turn >= inps) & (turn - inps < groups))
        def _():
            finish(turn - inps)
            spread(turn - inps)

        @pl.when(turn >= inps + 2)
        def _():
            hand_on(turn - inps - 2)

    @pl.loop(0, chans)
    def _(q):
        for r in range(1, inps):
            cross_copy(r, q).wait_send()

    for r in range(inps):
        deal_own(r).wait()

        @pl.loop(1, chans)
        def _(q):
            deal_copy(r, q).wait()

    @pl.loop(0, groups)
    def _(g):
        keep_copy(g).wait()
        spread_copy(None, g).wait()

        @pl.loop(1, chips)
        def _(p):
            spread_copy(p, g).wait_send()
            hand_copy(p, g).wait()

        @pl.loop(1, chans)
        def _(q):
            data_copy(g, q).wait_send()

        for d in range(1, inps):

            @pl.when(z < d)
            def _():
                up_copy(d, g).wait_send()

        for d in range(inps - 1):

            @pl.when(z > d)
            def _():
                down_copy(d, g).wait_send()


def exchange(mine, outgoing, delays, length_total, all_inputs):
    inps = outgoing.shape[0]
    chans, held, _, frames, width = mine.shape
    beams = delays.shape[1]
    groups = held // GROUP
    formed_shape = (held, chans * frames, 2 * beams // inps)
    dma = pltpu.SemaphoreType.DMA
    return pl.pallas_call(
        functools.partial(exchange_kernel, length_total, 1.0 / math.sqrt(all_inputs)),
        in_specs=[
            pl.BlockSpec(memory_space=pl.ANY),
            pl.BlockSpec(memory_space=pl.ANY),
            pl.BlockSpec(memory_space=pltpu.VMEM),
        ],
        out_specs=[
            pl.BlockSpec(memory_space=pl.ANY),
            pl.BlockSpec(memory_space=pl.ANY),
        ],
        out_shape=[
            jax.ShapeDtypeStruct(outgoing.shape, jnp.bfloat16),
            jax.ShapeDtypeStruct((chans, *formed_shape), jnp.bfloat16),
        ],
        scratch_shapes=[
            pltpu.VMEM(formed_shape, jnp.bfloat16),
            pltpu.VMEM(mine.shape, jnp.bfloat16),
            pltpu.VMEM(outgoing.shape, jnp.bfloat16),
            pltpu.VMEM((inps, *formed_shape), jnp.float32),
            pltpu.VMEM((inps, *formed_shape), jnp.bfloat16),
            pltpu.VMEM((inps, *formed_shape), jnp.bfloat16),
            pltpu.VMEM((inps, *formed_shape), jnp.bfloat16),
            pltpu.VMEM((2, width, beams), jnp.float32),
            pltpu.VMEM((2, width, beams), jnp.float32),
            dma((groups, chans)),
            dma((groups, chans)),
            dma((inps, chans)),
            dma((inps, chans)),
            dma((inps, chans)),
            dma((inps, chans)),
            dma((inps, groups)),
            dma((inps, groups)),
            dma((inps, groups)),
            dma((inps, groups)),
            dma((inps + 1,)),
            dma((chans // 2, groups)),
            dma((chans // 2, groups)),
            dma((chans // 2, groups)),
            dma((chans // 2, groups)),
            dma((groups,)),
        ],
        compiler_params=pltpu.CompilerParams(
            collective_id=0, has_side_effects=True, vmem_limit_bytes=VMEM_BYTES
        ),
        cost_estimate=pl.CostEstimate(
            flops=held * 2 * 4 * chans * frames * width * beams,
            bytes_accessed=held * chans * frames * (4 * width + 4 * beams),
            transcendentals=0,
        ),
    )(mine, outgoing, delays)


def shards(samples, gram_owner, beam_owner, delays, sections):
    input_count, frame_count, length_total = samples.shape
    half_count = length_total // 2
    inp_count = lax.axis_size("inp")
    chan_count = lax.axis_size("chan")
    inp_here = lax.axis_index("inp")
    chan_here = lax.axis_index("chan")
    all_inputs = input_count * inp_count
    all_frames = frame_count * chan_count
    owner_count = inp_count * chan_count
    gram_slots = 2 * gram_owner.shape[0] // owner_count
    beam_slots = 2 * half_count // chan_count
    held = half_count // chan_count
    table = fourier_table(length_total)
    spectra = jnp.einsum(
        "kpw,ifw->kpfi", table, samples, preferred_element_type=jnp.float32
    ).astype(jnp.bfloat16)

    mine = spectra.reshape(chan_count, held, 2, frame_count, input_count)
    gram_channel, gram_live = slot_table(gram_owner, owner_count, gram_slots)
    outgoing = jnp.take(spectra, gram_channel, axis=0, mode="clip").reshape(
        inp_count, chan_count, gram_slots, 2, frame_count, input_count
    )
    gram_live = gram_live.astype(jnp.int32).reshape(owner_count, gram_slots)
    gram_live = lax.dynamic_index_in_dim(gram_live, inp_here * chan_count + chan_here, 0, False)

    delay_cols = lax.dynamic_slice_in_dim(delays, inp_here * input_count, input_count, 1)
    ordered = jnp.take(delay_cols, sections, axis=0, mode="clip").T
    beam_channel, beam_live = slot_table(beam_owner, chan_count, beam_slots)
    here = lax.dynamic_slice_in_dim(beam_channel, chan_here * beam_slots, beam_slots)
    live = lax.dynamic_slice_in_dim(beam_live.astype(jnp.int32), chan_here * beam_slots, beam_slots)

    arrived, every = exchange(mine, outgoing, ordered, length_total, all_inputs)
    every = every.reshape(half_count, *every.shape[2:])
    visibilities, voltages = correlate(gram_live, arrived, all_frames, here, live, every)
    return (visibilities, voltages[:, None])


def solution(mesh):
    return jax.shard_map(
        shards,
        mesh=mesh,
        in_specs=(P("inp", "chan", None), P(), P(), P(), P()),
        out_specs=(P(("inp", "chan"), None, None, None), P("chan", "inp", None, None)),
        check_vma=False,
    )
```
